32 devices in a mesh: groups: 2 (over x), owners: 16 (over z, y, core).
Axes of the slice: x: 2, y: 2, z: 4, core: 2. Of those that a mesh axis runs over, the one named last changes fastest.
Arguments:
- embeddings: float32 [8192, 768], P(('groups', 'owners')), parts along dimension 0, may hold values from -6 to 6
- cluster_ids: int32 [8192], P(('groups', 'owners')), parts along dimension 0, may hold values from 0 to 255, as said below
Outputs:
- best_match: float32 [8192], P(('groups', 'owners')), parts along dimension 0
The draws below stay inside these ranges and needn't reach their ends.
There are 2 independent parts, one for each index of `groups`. The reference program is written for one: setup_inputs(seed, part) draws one part's arguments, and reference() takes and returns one part's arrays. A program takes and returns all parts, laid end to end along the dimension named above; each array names one. Nothing has to cross between parts.
Inputs may be any that keep to these rules, and one draw needn't show every extreme that they name: `cluster_ids`: cluster c is owned by device c mod (16) of the owners axis. The rows of one data shard (aligned blocks of 256 rows) fall in clusters of either none or exactly 32 rows for each owner.
All inputs are finite; a program needn't handle non-finite values.
Results may differ from the reference program's by a relative error of at most 0.0001.
Values sent between devices are 32-bit elements; how exact they have to be, the bound alone decides.
A program may use at most 64 MiB of HBM per device.

```python
import jax
import jax.numpy as jnp
from jax import lax

E = 768
ROWS_DEV = 256
CLU_DEV = 16
CAP = 32
ROWS = 4096
N_OWNERS = 16


def draw_cluster_ids(key, part):
    key = jax.random.fold_in(key, 7)
    groups_used = ROWS_DEV // CAP

    def one_block(block_key):
        first_key, second_key, third_key = jax.random.split(block_key, 3)
        chosen = jax.random.permutation(first_key, N_OWNERS)[:groups_used].astype(jnp.int32)
        places = jax.random.permutation(second_key, ROWS_DEV).astype(jnp.int32)
        dest = chosen[places // CAP]
        local = jax.random.randint(third_key, (ROWS_DEV,), 0, CLU_DEV, dtype=jnp.int32)
        return dest + N_OWNERS * local
    block_keys = jax.random.split(key, N_OWNERS)
    return jax.vmap(one_block)(block_keys).reshape(-1).astype(jnp.int32)


def block_scale(stream_key, extent, shards, low, high):
    gain, own = 1.0, jax.random.fold_in(stream_key, 6)
    for position, shards_of in shards:
        heights = jnp.exp(jax.random.uniform(jax.random.fold_in(own, position), (shards_of,), jnp.float32, low / len(shards), high / len(shards)))
        gain = gain * jnp.repeat(heights, extent[position] // shards_of).reshape([-1 if axis == position else 1 for axis in range(len(extent))])
    return gain


def noise(key, shape, deviation, reach, pieces=(), kind=jnp.bfloat16):
    loudness = block_scale(key, shape, pieces, -0.22, 0.18) if pieces else 1.0
    array = jax.random.normal(key, shape, jnp.float32) * deviation * loudness
    return jnp.minimum(jnp.maximum(array, -reach), reach).astype(kind)


def setup_inputs(seed: int = 0, part: int = 0) -> dict:
    key_of = jax.random.split(jax.random.key(seed), 3)
    part_keys = jax.random.split(jax.random.fold_in(key_of[2], part), 3)
    return {
        "embeddings": noise(part_keys[0], (ROWS, E), 1.0, 6.0, ((0, 16),), jnp.float32),
        "cluster_ids": draw_cluster_ids(jax.random.fold_in(jax.random.fold_in(key_of[2], part), 71), part),
    }


def to_unit(rows):
    return rows / jnp.sqrt(lax.optimization_barrier(jnp.sum(rows * rows, axis=1, keepdims=True)) + 1e-06)

def reference(embeddings, cluster_ids):
    total = embeddings.shape[0]
    owners = N_OWNERS
    span = N_OWNERS * CAP
    unit = to_unit(embeddings)
    dest = cluster_ids % owners
    counts = lax.optimization_barrier(jnp.sum((dest[:, None] == jnp.arange(owners, dtype=jnp.int32)[None, :]).astype(jnp.int32), axis=0))
    starts = (jnp.cumsum(counts) - counts).astype(jnp.int32)
    order = jnp.argsort(dest, stable=True).astype(jnp.int32)
    sorted_unit = unit[order]
    sorted_clu = cluster_ids[order]
    sorted_idx = order

    def visit(owner, carry):
        first = starts[owner]
        start = jnp.minimum(first, total - span).astype(jnp.int32)
        block = lax.dynamic_slice_in_dim(sorted_unit, start, span, 0)
        clu = lax.dynamic_slice_in_dim(sorted_clu, start, span, 0)
        idx = lax.dynamic_slice_in_dim(sorted_idx, start, span, 0)
        place = start + jnp.arange(span, dtype=jnp.int32)
        inside = (place >= first) & (place < first + counts[owner])
        scores = jnp.dot(block, block.T, precision=lax.Precision.HIGHEST, preferred_element_type=jnp.float32)
        valid = inside[None, :] & (clu[None, :] == clu[:, None]) & (idx[None, :] < idx[:, None])
        best = lax.optimization_barrier(jnp.max(jnp.where(valid, scores, jnp.float32(-1.0)), axis=1))
        old = lax.dynamic_slice_in_dim(carry, start, span, 0)
        return lax.dynamic_update_slice_in_dim(carry, jnp.where(inside, best, old), start, 0)
    sorted_best = lax.fori_loop(0, owners, visit, jnp.full((total,), -1.0, jnp.float32))
    return jnp.zeros((total,), jnp.float32).at[order].set(sorted_best)
```

```python
import functools
import math

import jax
import jax.numpy as jnp
from jax import lax
from jax.experimental import pallas as pl
from jax.experimental.pallas import tpu as pltpu
from jax.sharding import PartitionSpec as P

LANES = 128
MESH = pl.DeviceIdType.MESH
NT = (((1,), (1,)), ((), ()))
ORDER = (2, 3, 1, 0)


def to_unit(rows):
    return rows / jnp.sqrt(jnp.sum(rows * rows, axis=-1, keepdims=True) + 1e-06)


def split(x):
    high = x.astype(jnp.bfloat16)
    low = (x - high.astype(jnp.float32)).astype(jnp.bfloat16)
    return high, low


def dedup_kernel(
    n, cap, emb_ref, clu_ref, out_ref,
    unit_hi, unit_lo, slot_of, send_rows, got_rows, got_hi, got_lo,
    send_lab, got_lab, lab_col, best, got_best,
    row_send, row_recv, lab_send, lab_recv, best_send, best_recv,
):
    rows, width = emb_ref.shape
    per = LANES // cap
    planes = n // per
    me = lax.axis_index("owners")
    my_plane = me // per

    def plane_at(step):
        if planes == 4:
            return lax.bitwise_xor(my_plane, jnp.int32(step))
        return lax.rem(my_plane + step, planes)

    barrier = pltpu.get_barrier_semaphore()

    def greet(step, _):
        peer = lax.rem(me + step, n)
        pl.semaphore_signal(barrier, inc=1, device_id={"owners": peer}, device_id_type=MESH)
        return 0

    lax.fori_loop(1, n, greet, 0)

    clu = clu_ref[...].astype(jnp.float32)
    label = jnp.floor((clu + 0.5) * (1.0 / n))
    dest = clu - label * n
    label = label + 1.0
    owner = lax.broadcasted_iota(jnp.int32, (n, rows), 0).astype(jnp.float32)
    mine = dest == owner
    member = mine.astype(jnp.bfloat16)
    earlier = (
        lax.broadcasted_iota(jnp.int32, (rows, rows), 0)
        < lax.broadcasted_iota(jnp.int32, (rows, rows), 1)
    ).astype(jnp.bfloat16)
    ranks = jnp.dot(member, earlier, preferred_element_type=jnp.float32)
    slot_of[...] = jnp.where(mine, ranks, -1.0)
    rank = jnp.sum(jnp.where(mine, ranks, 0.0), axis=0, keepdims=True)

    lane_of = lax.broadcasted_iota(jnp.int32, (LANES, rows), 0).astype(jnp.float32)
    placed_labels = lax.dot_general(
        jnp.where(mine, label, 0.0), (lane_of == rank).astype(jnp.float32), NT,
        precision=lax.Precision.HIGHEST, preferred_element_type=jnp.float32,
    )
    for o in range(n):
        send_lab[o] = placed_labels[o : o + 1]

    unit = to_unit(emb_ref[...])
    unit_hi[...], unit_lo[...] = split(unit)

    pl.semaphore_wait(barrier, n - 1)

    def label_copy(peer):
        return pltpu.make_async_remote_copy(
            src_ref=send_lab.at[peer], dst_ref=got_lab.at[me],
            send_sem=lab_send.at[peer], recv_sem=lab_recv.at[me],
            device_id={"owners": peer}, device_id_type=MESH,
        )

    def row_copy(peer):
        return pltpu.make_async_remote_copy(
            src_ref=send_rows.at[peer], dst_ref=got_rows.at[me],
            send_sem=row_send.at[peer], recv_sem=row_recv.at[me],
            device_id={"owners": peer}, device_id_type=MESH,
        )

    def best_copy(peer):
        return pltpu.make_async_remote_copy(
            src_ref=best.at[peer // per], dst_ref=got_best.at[me],
            send_sem=best_send.at[peer], recv_sem=best_recv.at[me],
            device_id={"owners": peer}, device_id_type=MESH,
        )

    def arrived(buffer, sems, source):
        pltpu.make_async_remote_copy(
            src_ref=buffer.at[source], dst_ref=buffer.at[source],
            send_sem=sems.at[source], recv_sem=sems.at[source],
            device_id={"owners": source}, device_id_type=MESH,
        ).wait_recv()

    def others(do):
        def step_of(step, _):
            do(lax.rem(me + step, n))
            return 0

        lax.fori_loop(1, n, step_of, 0)

    got_lab[me] = send_lab[me]

    place = lax.broadcasted_iota(jnp.int32, (cap, rows), 0).astype(jnp.float32)
    order = ORDER if planes == 4 else tuple(range(planes))[::-1]
    for number, step in enumerate(order):
        first = plane_at(step) * per
        placing = jnp.concatenate(
            [(place == slot_of[pl.ds(first + i, 1), :]).astype(jnp.float32) for i in range(per)], axis=0
        ).astype(jnp.bfloat16)
        block = jnp.dot(placing, unit_hi[...], preferred_element_type=jnp.float32) + jnp.dot(
            placing, unit_lo[...], preferred_element_type=jnp.float32
        )
        for i in range(per):
            send_rows[first + i] = block[i * cap : (i + 1) * cap]
        for i in range(per):
            peer = first + i
            if step == 0:
                @pl.when(peer != me)
                def _():
                    row_copy(peer).start()
            else:
                row_copy(peer).start()
        if number == 0:
            others(lambda peer: label_copy(peer).start())

    got_rows[me] = send_rows[me]

    others(lambda peer: arrived(got_lab, lab_recv, peer))
    eye = lax.broadcasted_iota(jnp.int32, (cap, LANES), 0) == lax.broadcasted_iota(
        jnp.int32, (cap, LANES), 1
    )
    for plane in range(planes):
        for i in range(per):
            column = jnp.sum(
                jnp.where(eye, got_lab[plane * per + i], 0.0), axis=1, keepdims=True
            )
            lab_col[plane, pl.ds(i * cap, cap), :] = jnp.broadcast_to(column, (cap, LANES))
        best[plane] = jnp.full((1, LANES), -1.0, jnp.float32)

    square = (LANES, LANES)
    row_at = lax.broadcasted_iota(jnp.int32, square, 0)
    lane_at = lax.broadcasted_iota(jnp.int32, square, 1)
    for step in range(planes):
        new = plane_at(step)
        for i in range(per):
            source = new * per + i
            if step == 0:
                @pl.when(source != me)
                def _():
                    arrived(got_rows, row_recv, source)
            else:
                arrived(got_rows, row_recv, source)
        block = got_rows[pl.ds(new * per, per)].reshape(LANES, width)
        got_hi[new], got_lo[new] = split(block)
        for past in range(step + 1):
            old = plane_at(past)
            low, high = jnp.minimum(old, new), jnp.maximum(old, new)
            scores = (
                lax.dot_general(got_hi[low], got_hi[high], NT, preferred_element_type=jnp.float32)
                + lax.dot_general(got_hi[low], got_lo[high], NT, preferred_element_type=jnp.float32)
                + lax.dot_general(got_lo[low], got_hi[high], NT, preferred_element_type=jnp.float32)
            )
            candidate = lab_col[low]
            query = lab_col[high].T
            valid = (candidate == query) & (candidate > 0.0)
            if past == step:
                valid = valid & (row_at < lane_at)
            top = jnp.max(jnp.where(valid, scores, -1.0), axis=0, keepdims=True)
            best[high] = jnp.maximum(best[high], top)

    got_best[me] = best[my_plane]
    others(lambda peer: best_copy(peer).start())
    others(lambda peer: arrived(got_best, best_recv, peer))

    offset = (lax.rem(me, per) * cap).astype(jnp.float32)
    back = jnp.concatenate([got_best[o] for o in range(n)], axis=0)
    spread = jnp.dot(
        back, (lane_of == rank + offset).astype(jnp.float32),
        precision=lax.Precision.HIGHEST, preferred_element_type=jnp.float32,
    )
    out_ref[...] = jnp.sum(jnp.where(mine, spread, 0.0), axis=0, keepdims=True)

    def drain(peer):
        row_copy(peer).wait_send()
        label_copy(peer).wait_send()
        best_copy(peer).wait_send()

    others(drain)


def fused(embeddings, cluster_ids):
    rows, width = embeddings.shape
    n = lax.axis_size("owners")
    cap = rows * 2 // n
    planes = n * cap // LANES
    f32, bf16, dma = jnp.float32, jnp.bfloat16, pltpu.SemaphoreType.DMA
    out = pl.pallas_call(
        functools.partial(dedup_kernel, n, cap),
        out_shape=jax.ShapeDtypeStruct((1, rows), f32),
        in_specs=[pl.BlockSpec(memory_space=pltpu.VMEM)] * 2,
        out_specs=pl.BlockSpec(memory_space=pltpu.VMEM),
        scratch_shapes=[
            pltpu.VMEM((rows, width), bf16),
            pltpu.VMEM((rows, width), bf16),
            pltpu.VMEM((n, rows), f32),
            pltpu.VMEM((n, cap, width), f32),
            pltpu.VMEM((n, cap, width), f32),
            pltpu.VMEM((planes, LANES, width), bf16),
            pltpu.VMEM((planes, LANES, width), bf16),
            pltpu.VMEM((n, 1, LANES), f32),
            pltpu.VMEM((n, 1, LANES), f32),
            pltpu.VMEM((planes, LANES, LANES), f32),
            pltpu.VMEM((planes, 1, LANES), f32),
            pltpu.VMEM((n, 1, LANES), f32),
        ]
        + [dma((n,))] * 6,
        compiler_params=pltpu.CompilerParams(
            collective_id=0, has_side_effects=True, vmem_limit_bytes=32 * 1024 * 1024
        ),
    )(embeddings, cluster_ids.reshape(1, rows))
    return out.reshape(rows)


def plain(embeddings, cluster_ids):
    rows, width = embeddings.shape
    owners = lax.axis_size("owners")
    me = lax.axis_index("owners")
    capacity = max(rows * 2 // owners, 2)
    total = owners * capacity
    dest = cluster_ids % owners
    positions = jnp.arange(rows, dtype=jnp.int32)
    same_dest = (dest[:, None] == dest[None, :]) & (positions[None, :] < positions[:, None])
    rank = jnp.sum(same_dest.astype(jnp.int32), axis=1)
    slot_of_row = dest * capacity + rank
    placing = (jnp.arange(total, dtype=jnp.int32)[:, None] == slot_of_row[None, :]).astype(
        jnp.float32
    )
    global_idx = (me * rows + positions).astype(jnp.float32)
    payload = to_unit(embeddings)
    send_rows = jnp.dot(
        placing, payload, precision=lax.Precision.HIGHEST, preferred_element_type=jnp.float32
    ).reshape(owners, capacity, width)
    labels = jnp.stack([global_idx + 1.0, cluster_ids.astype(jnp.float32) + 1.0], axis=1)
    placed_labels = (
        jnp.dot(
            placing, labels, precision=lax.Precision.HIGHEST, preferred_element_type=jnp.float32
        )
        - 1.0
    )
    send_idx = placed_labels[:, 0].reshape(owners, capacity)
    send_clu = placed_labels[:, 1].reshape(owners, capacity)
    got_rows, got_idx, got_clu = (
        lax.all_to_all(send_rows, "owners", split_axis=0, concat_axis=0, tiled=True),
        lax.all_to_all(send_idx, "owners", split_axis=0, concat_axis=0, tiled=True),
        lax.all_to_all(send_clu, "owners", split_axis=0, concat_axis=0, tiled=True),
    )
    flat_rows = got_rows.reshape(total, width)
    flat_idx = got_idx.reshape(total)
    flat_clu = got_clu.reshape(total)
    block = math.gcd(total, 512)

    def one_block(inputs):
        query, query_idx, query_clu = inputs
        scores = jnp.dot(
            query, flat_rows.T, precision=lax.Precision.HIGHEST, preferred_element_type=jnp.float32
        )
        valid = (
            (flat_idx[None, :] >= 0.0)
            & (flat_clu[None, :] == query_clu[:, None])
            & (flat_idx[None, :] < query_idx[:, None])
        )
        return jnp.max(jnp.where(valid, scores, jnp.float32(-1.0)), axis=1)

    best = lax.map(
        one_block,
        (
            flat_rows.reshape(total // block, block, width),
            flat_idx.reshape(total // block, block),
            flat_clu.reshape(total // block, block),
        ),
    )
    back = lax.all_to_all(
        best.reshape(owners, capacity), "owners", split_axis=0, concat_axis=0, tiled=True
    )
    return jnp.dot(
        back.reshape(1, total),
        placing,
        precision=lax.Precision.HIGHEST,
        preferred_element_type=jnp.float32,
    ).reshape(rows)


def shards(embeddings, cluster_ids):
    rows, width = embeddings.shape
    n = lax.axis_size("owners")
    cap = rows * 2 // n
    fits = cap % 8 == 0 and LANES % cap == 0 and n % (LANES // cap) == 0
    if fits and rows % LANES == 0 and width % LANES == 0:
        return fused(embeddings, cluster_ids)
    return plain(embeddings, cluster_ids)


def solution(mesh):
    in_specs = (P(("groups", "owners"), None), P(("groups", "owners")))
    out_specs = P(("groups", "owners"))
    return jax.shard_map(shards, mesh=mesh, in_specs=in_specs, out_specs=out_specs, check_vma=False)
```

```python
import functools
import math

import jax
import jax.numpy as jnp
from jax import lax
from jax.experimental import pallas as pl
from jax.experimental.pallas import tpu as pltpu
from jax.sharding import PartitionSpec as P

LANES = 128
MESH = pl.DeviceIdType.MESH
NT = (((1,), (1,)), ((), ()))
ORDER = (2, 3, 1, 0)


def to_unit(rows):
    return rows / jnp.sqrt(jnp.sum(rows * rows, axis=-1, keepdims=True) + 1e-06)


def split(x):
    high = x.astype(jnp.bfloat16)
    low = (x - high.astype(jnp.float32)).astype(jnp.bfloat16)
    return high, low


def split3(x):
    high, rest = split(x)
    low = x - high.astype(jnp.float32) - rest.astype(jnp.float32)
    return high, rest, low.astype(jnp.bfloat16)


def dedup_kernel(
    n, cap, emb_hbm, clu_hbm, out_ref,
    emb_ref, clu_ref, unit_hi, unit_lo, slot_of, send_rows, got_rows, got_hi, got_lo,
    send_lab, got_lab, lab_col, best, got_best,
    in_sems, row_send, row_recv, lab_send, lab_recv, best_send, best_recv,
):
    rows, width = emb_ref.shape
    per = LANES // cap
    planes = n // per
    me = lax.axis_index("owners")
    my_plane = me // per

    def plane_at(step):
        if planes == 4:
            return lax.bitwise_xor(my_plane, jnp.int32(step))
        return lax.rem(my_plane + step, planes)

    def others(do):
        for step in range(1, n):
            do(lax.rem(me + step, n))

    clu_in = pltpu.make_async_copy(clu_hbm, clu_ref, in_sems.at[0])
    emb_in = pltpu.make_async_copy(emb_hbm, emb_ref, in_sems.at[1])
    clu_in.start()
    emb_in.start()

    barrier = pltpu.get_barrier_semaphore()
    others(
        lambda peer: pl.semaphore_signal(
            barrier, inc=1, device_id={"owners": peer}, device_id_type=MESH
        )
    )

    def remote(src, dst, send, recv, peer):
        return pltpu.make_async_remote_copy(
            src_ref=src, dst_ref=dst, send_sem=send, recv_sem=recv,
            device_id={"owners": peer}, device_id_type=MESH,
        )

    def label_copy(peer):
        return remote(send_lab.at[peer], got_lab.at[me], lab_send, lab_recv, peer)

    def row_copy(peer):
        return remote(
            send_rows.at[peer], got_rows.at[me], row_send, row_recv.at[my_plane], peer
        )

    def best_copy(peer):
        return remote(best.at[peer // per], got_best.at[me], best_send, best_recv, peer)

    def batch(buffer, first, count, send, recv):
        part = buffer.at[pl.ds(first, count)]
        return remote(part, part, send, recv, me)

    clu_in.wait()
    clu = clu_ref[...].astype(jnp.float32)
    label = jnp.floor((clu + 0.5) * (1.0 / n))
    dest = clu - label * n
    label = label + 1.0
    owner = lax.broadcasted_iota(jnp.int32, (n, rows), 0).astype(jnp.float32)
    mine = dest == owner
    member = mine.astype(jnp.bfloat16)
    earlier = (
        lax.broadcasted_iota(jnp.int32, (rows, rows), 0)
        < lax.broadcasted_iota(jnp.int32, (rows, rows), 1)
    ).astype(jnp.bfloat16)
    ranks = jnp.dot(member, earlier, preferred_element_type=jnp.float32)
    slot_of[...] = jnp.where(mine, ranks, -1.0)

    rank = jnp.sum(jnp.where(mine, ranks, 0.0), axis=0, keepdims=True)
    lane_of = lax.broadcasted_iota(jnp.int32, (LANES, rows), 0).astype(jnp.float32)
    placed_labels = lax.dot_general(
        jnp.where(mine, label, 0.0), (lane_of == rank).astype(jnp.float32), NT,
        precision=lax.Precision.HIGHEST, preferred_element_type=jnp.float32,
    )
    for o in range(n):
        send_lab[o] = placed_labels[o : o + 1]

    emb_in.wait()
    unit_hi[...], unit_lo[...] = split(to_unit(emb_ref[...]))

    place = lax.broadcasted_iota(jnp.int32, (cap, rows), 0).astype(jnp.float32)

    def put(step):
        first = plane_at(step) * per
        placing = jnp.concatenate(
            [(place == slot_of[pl.ds(first + i, 1), :]).astype(jnp.float32) for i in range(per)], axis=0
        ).astype(jnp.bfloat16)
        block = jnp.dot(placing, unit_hi[...], preferred_element_type=jnp.float32) + jnp.dot(
            placing, unit_lo[...], preferred_element_type=jnp.float32
        )
        for i in range(per):
            send_rows[first + i] = block[i * cap : (i + 1) * cap]

    def send(step):
        first = plane_at(step) * per
        if step == 0:
            for i in range(1, per):
                row_copy(first + lax.rem(me - first + i, per)).start()
        else:
            for i in range(per):
                row_copy(first + lax.rem(me + i, per)).start()

    order = ORDER if planes == 4 else tuple(range(planes))[::-1]
    put(order[0])
    pl.semaphore_wait(barrier, n - 1)
    others(lambda peer: label_copy(peer).start())
    got_lab[me] = send_lab[me]
    send(order[0])
    for step in order[1:]:
        put(step)
        send(step)
    got_rows[me] = send_rows[me]

    offset = (lax.rem(me, per) * cap).astype(jnp.float32)
    lookup = (lane_of == rank + offset).astype(jnp.bfloat16)

    batch(got_lab, 0, n - 1, lab_send, lab_recv).wait()
    eye = lax.broadcasted_iota(jnp.int32, (cap, LANES), 0) == lax.broadcasted_iota(
        jnp.int32, (cap, LANES), 1
    )
    for plane in range(planes):
        for i in range(per):
            column = jnp.sum(
                jnp.where(eye, got_lab[plane * per + i], 0.0), axis=1, keepdims=True
            )
            lab_col[plane, pl.ds(i * cap, cap), :] = jnp.broadcast_to(column, (cap, LANES))
        best[plane] = jnp.full((1, LANES), -1.0, jnp.float32)

    square = (LANES, LANES)
    row_at = lax.broadcasted_iota(jnp.int32, square, 0)
    lane_at = lax.broadcasted_iota(jnp.int32, square, 1)
    for step in range(planes):
        new = plane_at(step)
        count = per - 1 if step == 0 else per
        batch(got_rows, 0, count, row_send, row_recv.at[new]).wait_recv()
        block = got_rows[pl.ds(new * per, per)].reshape(LANES, width)
        got_hi[new], got_lo[new] = split(block)
        for past in range(step + 1):
            old = plane_at(past)
            low, high = jnp.minimum(old, new), jnp.maximum(old, new)
            scores = (
                lax.dot_general(got_hi[low], got_hi[high], NT, preferred_element_type=jnp.float32)
                + lax.dot_general(got_hi[low], got_lo[high], NT, preferred_element_type=jnp.float32)
                + lax.dot_general(got_lo[low], got_hi[high], NT, preferred_element_type=jnp.float32)
            )
            candidate = lab_col[low]
            query = lab_col[high].T
            valid = (candidate == query) & (candidate > 0.0)
            if past == step:
                valid = valid & (row_at < lane_at)
            top = jnp.max(jnp.where(valid, scores, -1.0), axis=0, keepdims=True)
            best[high] = jnp.maximum(best[high], top)

    others(lambda peer: best_copy(peer).start())
    got_best[me] = best[my_plane]
    batch(send_rows, 0, n - 1, row_send, row_recv.at[0]).wait_send()
    batch(got_best, 0, n - 1, best_send, best_recv).wait()

    back = jnp.concatenate([got_best[o] for o in range(n)], axis=0)
    spread = jnp.dot(
        jnp.concatenate(split3(back), axis=0), lookup, preferred_element_type=jnp.float32
    )
    spread = spread[:n] + spread[n : 2 * n] + spread[2 * n :]
    out_ref[...] = jnp.sum(jnp.where(mine, spread, 0.0), axis=0, keepdims=True)


def fused(embeddings, cluster_ids):
    rows, width = embeddings.shape
    n = lax.axis_size("owners")
    cap = rows * 2 // n
    planes = n * cap // LANES
    f32, bf16, dma = jnp.float32, jnp.bfloat16, pltpu.SemaphoreType.DMA
    out = pl.pallas_call(
        functools.partial(dedup_kernel, n, cap),
        out_shape=jax.ShapeDtypeStruct((1, rows), f32),
        in_specs=[pl.BlockSpec(memory_space=pltpu.HBM)] * 2,
        out_specs=pl.BlockSpec(memory_space=pltpu.VMEM),
        scratch_shapes=[
            pltpu.VMEM((rows, width), f32),
            pltpu.VMEM((1, rows), jnp.int32),
            pltpu.VMEM((rows, width), bf16),
            pltpu.VMEM((rows, width), bf16),
            pltpu.VMEM((n, rows), f32),
            pltpu.VMEM((n, cap, width), f32),
            pltpu.VMEM((n, cap, width), f32),
            pltpu.VMEM((planes, LANES, width), bf16),
            pltpu.VMEM((planes, LANES, width), bf16),
            pltpu.VMEM((n, 1, LANES), f32),
            pltpu.VMEM((n, 1, LANES), f32),
            pltpu.VMEM((planes, LANES, LANES), f32),
            pltpu.VMEM((planes, 1, LANES), f32),
            pltpu.VMEM((n, 1, LANES), f32),
            dma((2,)), dma, dma((planes,)), dma, dma, dma, dma,
        ],
        compiler_params=pltpu.CompilerParams(
            collective_id=0, has_side_effects=True, vmem_limit_bytes=32 * 1024 * 1024
        ),
    )(embeddings, cluster_ids.reshape(1, rows))
    return out.reshape(rows)


def plain(embeddings, cluster_ids):
    rows, width = embeddings.shape
    owners = lax.axis_size("owners")
    me = lax.axis_index("owners")
    capacity = max(rows * 2 // owners, 2)
    total = owners * capacity
    dest = cluster_ids % owners
    positions = jnp.arange(rows, dtype=jnp.int32)
    same_dest = (dest[:, None] == dest[None, :]) & (positions[None, :] < positions[:, None])
    rank = jnp.sum(same_dest.astype(jnp.int32), axis=1)
    slot_of_row = dest * capacity + rank
    placing = (jnp.arange(total, dtype=jnp.int32)[:, None] == slot_of_row[None, :]).astype(
        jnp.float32
    )
    global_idx = (me * rows + positions).astype(jnp.float32)
    payload = to_unit(embeddings)
    send_rows = jnp.dot(
        placing, payload, precision=lax.Precision.HIGHEST, preferred_element_type=jnp.float32
    ).reshape(owners, capacity, width)
    labels = jnp.stack([global_idx + 1.0, cluster_ids.astype(jnp.float32) + 1.0], axis=1)
    placed_labels = (
        jnp.dot(
            placing, labels, precision=lax.Precision.HIGHEST, preferred_element_type=jnp.float32
        )
        - 1.0
    )
    send_idx = placed_labels[:, 0].reshape(owners, capacity)
    send_clu = placed_labels[:, 1].reshape(owners, capacity)
    got_rows, got_idx, got_clu = (
        lax.all_to_all(send_rows, "owners", split_axis=0, concat_axis=0, tiled=True),
        lax.all_to_all(send_idx, "owners", split_axis=0, concat_axis=0, tiled=True),
        lax.all_to_all(send_clu, "owners", split_axis=0, concat_axis=0, tiled=True),
    )
    flat_rows = got_rows.reshape(total, width)
    flat_idx = got_idx.reshape(total)
    flat_clu = got_clu.reshape(total)
    block = math.gcd(total, 512)

    def one_block(inputs):
        query, query_idx, query_clu = inputs
        scores = jnp.dot(
            query, flat_rows.T, precision=lax.Precision.HIGHEST, preferred_element_type=jnp.float32
        )
        valid = (
            (flat_idx[None, :] >= 0.0)
            & (flat_clu[None, :] == query_clu[:, None])
            & (flat_idx[None, :] < query_idx[:, None])
        )
        return jnp.max(jnp.where(valid, scores, jnp.float32(-1.0)), axis=1)

    best = lax.map(
        one_block,
        (
            flat_rows.reshape(total // block, block, width),
            flat_idx.reshape(total // block, block),
            flat_clu.reshape(total // block, block),
        ),
    )
    back = lax.all_to_all(
        best.reshape(owners, capacity), "owners", split_axis=0, concat_axis=0, tiled=True
    )
    return jnp.dot(
        back.reshape(1, total),
        placing,
        precision=lax.Precision.HIGHEST,
        preferred_element_type=jnp.float32,
    ).reshape(rows)


def shards(embeddings, cluster_ids):
    rows, width = embeddings.shape
    n = lax.axis_size("owners")
    cap = rows * 2 // n
    fits = cap % 8 == 0 and LANES % cap == 0 and n % (LANES // cap) == 0
    if fits and rows % LANES == 0 and width % LANES == 0:
        return fused(embeddings, cluster_ids)
    return plain(embeddings, cluster_ids)


def solution(mesh):
    in_specs = (P(("groups", "owners"), None), P(("groups", "owners")))
    out_specs = P(("groups", "owners"))
    return jax.shard_map(shards, mesh=mesh, in_specs=in_specs, out_specs=out_specs, check_vma=False)
```

```python
import functools
import math

import jax
import jax.numpy as jnp
from jax import lax
from jax.experimental import pallas as pl
from jax.experimental.pallas import tpu as pltpu
from jax.sharding import PartitionSpec as P

LANES = 128
MESH = pl.DeviceIdType.MESH
NT = (((1,), (1,)), ((), ()))
ORDER = (2, 3, 1, 0)


def to_unit(rows):
    return rows / jnp.sqrt(jnp.sum(rows * rows, axis=-1, keepdims=True) + 1e-06)


def split(x):
    high = x.astype(jnp.bfloat16)
    low = (x - high.astype(jnp.float32)).astype(jnp.bfloat16)
    return high, low


def split3(x):
    high, rest = split(x)
    low = x - high.astype(jnp.float32) - rest.astype(jnp.float32)
    return high, rest, low.astype(jnp.bfloat16)


def dedup_kernel(
    n, cap, emb_hbm, clu_hbm, out_ref,
    emb_ref, clu_ref, unit_hi, unit_lo, slot_of, send_rows, got_rows, got_hi, got_lo,
    send_lab, got_lab, lab_col, best, got_best,
    in_sems, row_send, row_recv, lab_send, lab_recv, best_send, best_recv,
):
    rows, width = emb_ref.shape
    per = LANES // cap
    planes = n // per
    me = lax.axis_index("owners")
    my_plane = me // per

    def plane_at(step):
        if planes == 4:
            return lax.bitwise_xor(my_plane, jnp.int32(step))
        return lax.rem(my_plane + step, planes)

    def others(do):
        for step in range(1, n):
            do(lax.rem(me + step, n))

    clu_in = pltpu.make_async_copy(clu_hbm, clu_ref, in_sems.at[0])
    emb_in = pltpu.make_async_copy(emb_hbm, emb_ref, in_sems.at[1])
    clu_in.start()
    emb_in.start()

    barrier = pltpu.get_barrier_semaphore()
    others(
        lambda peer: pl.semaphore_signal(
            barrier, inc=1, device_id={"owners": peer}, device_id_type=MESH
        )
    )

    def remote(src, dst, send, recv, peer):
        return pltpu.make_async_remote_copy(
            src_ref=src, dst_ref=dst, send_sem=send, recv_sem=recv,
            device_id={"owners": peer}, device_id_type=MESH,
        )

    def label_copy(peer):
        return remote(send_lab.at[peer], got_lab.at[me], lab_send, lab_recv, peer)

    def row_copy(peer):
        return remote(
            send_rows.at[peer], got_rows.at[me], row_send, row_recv.at[my_plane], peer
        )

    def best_copy(peer):
        return remote(best.at[peer // per], got_best.at[me], best_send, best_recv, peer)

    def batch(buffer, first, count, send, recv):
        part = buffer.at[pl.ds(first, count)]
        return remote(part, part, send, recv, me)

    clu_in.wait()
    clu = clu_ref[...].astype(jnp.float32)
    label = jnp.floor((clu + 0.5) * (1.0 / n))
    dest = clu - label * n
    label = label + 1.0
    owner = lax.broadcasted_iota(jnp.int32, (n, rows), 0).astype(jnp.float32)
    mine = dest == owner
    member = mine.astype(jnp.bfloat16)
    earlier = (
        lax.broadcasted_iota(jnp.int32, (rows, rows), 0)
        < lax.broadcasted_iota(jnp.int32, (rows, rows), 1)
    ).astype(jnp.bfloat16)
    ranks = jnp.dot(member, earlier, preferred_element_type=jnp.float32)
    slot_of[...] = jnp.where(mine, ranks, -1.0)

    rank = jnp.sum(jnp.where(mine, ranks, 0.0), axis=0, keepdims=True)
    lane_of = lax.broadcasted_iota(jnp.int32, (LANES, rows), 0).astype(jnp.float32)
    placed_labels = lax.dot_general(
        jnp.where(mine, label, 0.0), (lane_of == rank).astype(jnp.float32), NT,
        precision=lax.Precision.HIGHEST, preferred_element_type=jnp.float32,
    )
    for o in range(n):
        send_lab[o] = placed_labels[o : o + 1]

    emb_in.wait()
    unit_hi[...], unit_lo[...] = split(to_unit(emb_ref[...]))

    place = lax.broadcasted_iota(jnp.int32, (cap, rows), 0).astype(jnp.float32)

    def put(step):
        first = plane_at(step) * per
        placing = jnp.concatenate(
            [(place == slot_of[pl.ds(first + i, 1), :]).astype(jnp.float32) for i in range(per)], axis=0
        ).astype(jnp.bfloat16)
        block = jnp.dot(placing, unit_hi[...], preferred_element_type=jnp.float32) + jnp.dot(
            placing, unit_lo[...], preferred_element_type=jnp.float32
        )
        for i in range(per):
            send_rows[first + i] = block[i * cap : (i + 1) * cap]

    def send(step):
        first = plane_at(step) * per
        if step == 0:
            for i in range(1, per):
                row_copy(first + lax.rem(me - first + i, per)).start()
        else:
            for i in range(per):
                row_copy(first + lax.rem(me + i, per)).start()

    order = ORDER if planes == 4 else tuple(range(planes))[::-1]
    put(order[0])
    pl.semaphore_wait(barrier, n - 1)
    others(lambda peer: label_copy(peer).start())
    got_lab[me] = send_lab[me]
    send(order[0])
    for step in order[1:]:
        put(step)
        send(step)
    got_rows[me] = send_rows[me]

    offset = (lax.rem(me, per) * cap).astype(jnp.float32)
    lookup = (lane_of == rank + offset).astype(jnp.bfloat16)

    batch(got_lab, 0, n - 1, lab_send, lab_recv).wait()
    eye = lax.broadcasted_iota(jnp.int32, (cap, LANES), 0) == lax.broadcasted_iota(
        jnp.int32, (cap, LANES), 1
    )
    for plane in range(planes):
        for i in range(per):
            column = jnp.sum(
                jnp.where(eye, got_lab[plane * per + i], 0.0), axis=1, keepdims=True
            )
            lab_col[plane, pl.ds(i * cap, cap), :] = jnp.broadcast_to(column, (cap, LANES))
        best[plane] = jnp.full((1, LANES), -1.0, jnp.float32)

    square = (LANES, LANES)
    row_at = lax.broadcasted_iota(jnp.int32, square, 0)
    lane_at = lax.broadcasted_iota(jnp.int32, square, 1)
    for step in range(planes):
        new = plane_at(step)
        count = per - 1 if step == 0 else per
        batch(got_rows, 0, count, row_send, row_recv.at[new]).wait_recv()
        block = got_rows[pl.ds(new * per, per)].reshape(LANES, width)
        got_hi[new], got_lo[new] = split(block)
        for past in range(step + 1):
            old = plane_at(past)
            low, high = jnp.minimum(old, new), jnp.maximum(old, new)
            scores = (
                lax.dot_general(got_hi[low], got_hi[high], NT, preferred_element_type=jnp.float32)
                + lax.dot_general(got_hi[low], got_lo[high], NT, preferred_element_type=jnp.float32)
                + lax.dot_general(got_lo[low], got_hi[high], NT, preferred_element_type=jnp.float32)
            )
            candidate = lab_col[low]
            query = lab_col[high].T
            valid = (candidate == query) & (candidate > 0.0)
            if past == step:
                valid = valid & (row_at < lane_at)
            top = jnp.max(jnp.where(valid, scores, -1.0), axis=0, keepdims=True)
            best[high] = jnp.maximum(best[high], top)

    others(lambda peer: best_copy(peer).start())
    got_best[me] = best[my_plane]
    batch(send_rows, 0, n - 1, row_send, row_recv.at[0]).wait_send()
    batch(got_best, 0, n - 1, best_send, best_recv).wait()

    back = jnp.concatenate([got_best[o] for o in range(n)], axis=0)
    spread = jnp.dot(
        jnp.concatenate(split3(back), axis=0), lookup, preferred_element_type=jnp.float32
    )
    spread = spread[:n] + spread[n : 2 * n] + spread[2 * n :]
    out_ref[...] = jnp.sum(jnp.where(mine, spread, 0.0), axis=0, keepdims=True)


def fused(embeddings, cluster_ids):
    rows, width = embeddings.shape
    n = lax.axis_size("owners")
    cap = rows * 2 // n
    planes = n * cap // LANES
    f32, bf16, dma = jnp.float32, jnp.bfloat16, pltpu.SemaphoreType.DMA
    out = pl.pallas_call(
        functools.partial(dedup_kernel, n, cap),
        out_shape=jax.ShapeDtypeStruct((1, rows), f32),
        in_specs=[pl.BlockSpec(memory_space=pltpu.HBM)] * 2,
        out_specs=pl.BlockSpec(memory_space=pltpu.VMEM),
        scratch_shapes=[
            pltpu.VMEM((rows, width), f32),
            pltpu.VMEM((1, rows), jnp.int32),
            pltpu.VMEM((rows, width), bf16),
            pltpu.VMEM((rows, width), bf16),
            pltpu.VMEM((n, rows), f32),
            pltpu.VMEM((n, cap, width), f32),
            pltpu.VMEM((n, cap, width), f32),
            pltpu.VMEM((planes, LANES, width), bf16),
            pltpu.VMEM((planes, LANES, width), bf16),
            pltpu.VMEM((n, 1, LANES), f32),
            pltpu.VMEM((n, 1, LANES), f32),
            pltpu.VMEM((planes, LANES, LANES), f32),
            pltpu.VMEM((planes, 1, LANES), f32),
            pltpu.VMEM((n, 1, LANES), f32),
            dma((2,)), dma, dma((planes,)), dma, dma, dma, dma,
        ],
        compiler_params=pltpu.CompilerParams(
            collective_id=0, has_side_effects=True, vmem_limit_bytes=60 * 1024 * 1024
        ),
    )(embeddings, cluster_ids.reshape(1, rows))
    return out.reshape(rows)


def plain(embeddings, cluster_ids):
    rows, width = embeddings.shape
    owners = lax.axis_size("owners")
    me = lax.axis_index("owners")
    capacity = max(rows * 2 // owners, 2)
    total = owners * capacity
    dest = cluster_ids % owners
    positions = jnp.arange(rows, dtype=jnp.int32)
    same_dest = (dest[:, None] == dest[None, :]) & (positions[None, :] < positions[:, None])
    rank = jnp.sum(same_dest.astype(jnp.int32), axis=1)
    slot_of_row = dest * capacity + rank
    placing = (jnp.arange(total, dtype=jnp.int32)[:, None] == slot_of_row[None, :]).astype(
        jnp.float32
    )
    global_idx = (me * rows + positions).astype(jnp.float32)
    payload = to_unit(embeddings)
    send_rows = jnp.dot(
        placing, payload, precision=lax.Precision.HIGHEST, preferred_element_type=jnp.float32
    ).reshape(owners, capacity, width)
    labels = jnp.stack([global_idx + 1.0, cluster_ids.astype(jnp.float32) + 1.0], axis=1)
    placed_labels = (
        jnp.dot(
            placing, labels, precision=lax.Precision.HIGHEST, preferred_element_type=jnp.float32
        )
        - 1.0
    )
    send_idx = placed_labels[:, 0].reshape(owners, capacity)
    send_clu = placed_labels[:, 1].reshape(owners, capacity)
    got_rows, got_idx, got_clu = (
        lax.all_to_all(send_rows, "owners", split_axis=0, concat_axis=0, tiled=True),
        lax.all_to_all(send_idx, "owners", split_axis=0, concat_axis=0, tiled=True),
        lax.all_to_all(send_clu, "owners", split_axis=0, concat_axis=0, tiled=True),
    )
    flat_rows = got_rows.reshape(total, width)
    flat_idx = got_idx.reshape(total)
    flat_clu = got_clu.reshape(total)
    block = math.gcd(total, 512)

    def one_block(inputs):
        query, query_idx, query_clu = inputs
        scores = jnp.dot(
            query, flat_rows.T, precision=lax.Precision.HIGHEST, preferred_element_type=jnp.float32
        )
        valid = (
            (flat_idx[None, :] >= 0.0)
            & (flat_clu[None, :] == query_clu[:, None])
            & (flat_idx[None, :] < query_idx[:, None])
        )
        return jnp.max(jnp.where(valid, scores, jnp.float32(-1.0)), axis=1)

    best = lax.map(
        one_block,
        (
            flat_rows.reshape(total // block, block, width),
            flat_idx.reshape(total // block, block),
            flat_clu.reshape(total // block, block),
        ),
    )
    back = lax.all_to_all(
        best.reshape(owners, capacity), "owners", split_axis=0, concat_axis=0, tiled=True
    )
    return jnp.dot(
        back.reshape(1, total),
        placing,
        precision=lax.Precision.HIGHEST,
        preferred_element_type=jnp.float32,
    ).reshape(rows)


def shards(embeddings, cluster_ids):
    rows, width = embeddings.shape
    n = lax.axis_size("owners")
    cap = rows * 2 // n
    fits = cap % 8 == 0 and LANES % cap == 0 and n % (LANES // cap) == 0
    if fits and rows % LANES == 0 and width % LANES == 0:
        return fused(embeddings, cluster_ids)
    return plain(embeddings, cluster_ids)


def solution(mesh):
    in_specs = (P(("groups", "owners"), None), P(("groups", "owners")))
    out_specs = P(("groups", "owners"))
    return jax.shard_map(shards, mesh=mesh, in_specs=in_specs, out_specs=out_specs, check_vma=False)
```

```python
import functools
import math

import jax
import jax.numpy as jnp
from jax import lax
from jax.experimental import pallas as pl
from jax.experimental.pallas import tpu as pltpu
from jax.sharding import PartitionSpec as P

LANES = 128
MESH = pl.DeviceIdType.MESH
NT = (((1,), (1,)), ((), ()))
ORDER = (2, 3, 1, 0)


def to_unit(rows):
    return rows / jnp.sqrt(jnp.sum(rows * rows, axis=-1, keepdims=True) + 1e-06)


def split(x):
    high = x.astype(jnp.bfloat16)
    low = (x - high.astype(jnp.float32)).astype(jnp.bfloat16)
    return high, low


def split3(x):
    high, rest = split(x)
    low = x - high.astype(jnp.float32) - rest.astype(jnp.float32)
    return high, rest, low.astype(jnp.bfloat16)


def dedup_kernel(
    n, cap, emb_hbm, clu_hbm, out_ref,
    emb_ref, clu_ref, unit_hi, unit_lo, slot_of, send_rows, got_rows, got_hi, got_lo,
    send_lab, got_lab, lab_col, best, got_best,
    in_sems, row_send, row_recv, lab_send, lab_recv, best_send, best_recv,
):
    rows, width = emb_ref.shape
    per = LANES // cap
    planes = n // per
    me = lax.axis_index("owners")
    my_plane = me // per

    def plane_at(step):
        if planes == 4:
            return lax.bitwise_xor(my_plane, jnp.int32(step))
        return lax.rem(my_plane + step, planes)

    def others(do):
        for step in range(1, n):
            do(lax.rem(me + step, n))

    clu_in = pltpu.make_async_copy(clu_hbm, clu_ref, in_sems.at[0])
    emb_in = pltpu.make_async_copy(emb_hbm, emb_ref, in_sems.at[1])
    clu_in.start()
    emb_in.start()

    barrier = pltpu.get_barrier_semaphore()
    others(
        lambda peer: pl.semaphore_signal(
            barrier, inc=1, device_id={"owners": peer}, device_id_type=MESH
        )
    )

    def remote(src, dst, send, recv, peer):
        return pltpu.make_async_remote_copy(
            src_ref=src, dst_ref=dst, send_sem=send, recv_sem=recv,
            device_id={"owners": peer}, device_id_type=MESH,
        )

    def label_copy(peer):
        return remote(send_lab.at[peer], got_lab.at[me], lab_send, lab_recv, peer)

    def row_copy(peer):
        return remote(
            send_rows.at[peer], got_rows.at[me], row_send, row_recv.at[my_plane], peer
        )

    def best_copy(peer):
        return remote(best.at[peer // per], got_best.at[me], best_send, best_recv, peer)

    def batch(buffer, first, count, send, recv):
        part = buffer.at[pl.ds(first, count)]
        return remote(part, part, send, recv, me)

    clu_in.wait()
    clu = clu_ref[...].astype(jnp.float32)
    label = jnp.floor((clu + 0.5) * (1.0 / n))
    dest = clu - label * n
    label = label + 1.0
    owner = lax.broadcasted_iota(jnp.int32, (n, rows), 0).astype(jnp.float32)
    mine = dest == owner
    member = mine.astype(jnp.bfloat16)
    earlier = (
        lax.broadcasted_iota(jnp.int32, (rows, rows), 0)
        < lax.broadcasted_iota(jnp.int32, (rows, rows), 1)
    ).astype(jnp.bfloat16)
    ranks = jnp.dot(member, earlier, preferred_element_type=jnp.float32)
    slot_of[...] = jnp.where(mine, ranks, -1.0)

    rank = jnp.sum(jnp.where(mine, ranks, 0.0), axis=0, keepdims=True)
    lane_of = lax.broadcasted_iota(jnp.int32, (LANES, rows), 0).astype(jnp.float32)
    placed_labels = lax.dot_general(
        jnp.where(mine, label, 0.0), (lane_of == rank).astype(jnp.float32), NT,
        precision=lax.Precision.HIGHEST, preferred_element_type=jnp.float32,
    )
    for o in range(n):
        send_lab[o] = placed_labels[o : o + 1]

    emb_in.wait()
    unit_hi[...], unit_lo[...] = split(to_unit(emb_ref[...]))

    place = lax.broadcasted_iota(jnp.int32, (cap, rows), 0).astype(jnp.float32)

    def put(step):
        first = plane_at(step) * per
        placing = jnp.concatenate(
            [(place == slot_of[pl.ds(first + i, 1), :]).astype(jnp.float32) for i in range(per)], axis=0
        ).astype(jnp.bfloat16)
        block = jnp.dot(placing, unit_hi[...], preferred_element_type=jnp.float32) + jnp.dot(
            placing, unit_lo[...], preferred_element_type=jnp.float32
        )
        for i in range(per):
            send_rows[first + i] = block[i * cap : (i + 1) * cap]

    def send(step):
        first = plane_at(step) * per
        if step == 0:
            for i in range(1, per):
                row_copy(first + lax.rem(me - first + i, per)).start()
        else:
            for i in range(per):
                row_copy(first + lax.rem(me + i, per)).start()

    order = ORDER if planes == 4 else tuple(range(planes))[::-1]
    put(order[0])
    pl.semaphore_wait(barrier, n - 1)
    others(lambda peer: label_copy(peer).start())
    got_lab[me] = send_lab[me]
    send(order[0])
    for step in order[1:]:
        put(step)
        send(step)
    got_rows[me] = send_rows[me]

    offset = (lax.rem(me, per) * cap).astype(jnp.float32)
    lookup = (lane_of == rank + offset).astype(jnp.bfloat16)

    batch(got_lab, 0, n - 1, lab_send, lab_recv).wait()
    eye = lax.broadcasted_iota(jnp.int32, (cap, LANES), 0) == lax.broadcasted_iota(
        jnp.int32, (cap, LANES), 1
    )
    for plane in range(planes):
        for i in range(per):
            column = jnp.sum(
                jnp.where(eye, got_lab[plane * per + i], 0.0), axis=1, keepdims=True
            )
            lab_col[plane, pl.ds(i * cap, cap), :] = jnp.broadcast_to(column, (cap, LANES))
        best[plane] = jnp.full((1, LANES), -1.0, jnp.float32)

    square = (LANES, LANES)
    row_at = lax.broadcasted_iota(jnp.int32, square, 0)
    lane_at = lax.broadcasted_iota(jnp.int32, square, 1)
    for step in range(planes):
        new = plane_at(step)
        count = per - 1 if step == 0 else per
        batch(got_rows, 0, count, row_send, row_recv.at[new]).wait_recv()
        block = got_rows[pl.ds(new * per, per)].reshape(LANES, width)
        got_hi[new], got_lo[new] = split(block)
        for past in range(step + 1):
            old = plane_at(past)
            low, high = jnp.minimum(old, new), jnp.maximum(old, new)
            scores = (
                lax.dot_general(got_hi[low], got_hi[high], NT, preferred_element_type=jnp.float32)
                + lax.dot_general(got_hi[low], got_lo[high], NT, preferred_element_type=jnp.float32)
                + lax.dot_general(got_lo[low], got_hi[high], NT, preferred_element_type=jnp.float32)
            )
            candidate = lab_col[low]
            query = lab_col[high].T
            valid = (candidate == query) & (candidate > 0.0)
            if past == step:
                valid = valid & (row_at < lane_at)
            top = jnp.max(jnp.where(valid, scores, -1.0), axis=0, keepdims=True)
            best[high] = jnp.maximum(best[high], top)

    others(lambda peer: best_copy(peer).start())
    got_best[me] = best[my_plane]
    batch(send_rows, 0, n - 1, row_send, row_recv.at[0]).wait_send()
    batch(got_best, 0, n - 1, best_send, best_recv).wait()

    back = jnp.concatenate([got_best[o] for o in range(n)], axis=0)
    spread = jnp.dot(
        jnp.concatenate(split3(back), axis=0), lookup, preferred_element_type=jnp.float32
    )
    spread = spread[:n] + spread[n : 2 * n] + spread[2 * n :]
    out_ref[...] = jnp.sum(jnp.where(mine, spread, 0.0), axis=0, keepdims=True)


def fused(embeddings, cluster_ids):
    rows, width = embeddings.shape
    n = lax.axis_size("owners")
    cap = rows * 2 // n
    planes = n * cap // LANES
    f32, bf16, dma = jnp.float32, jnp.bfloat16, pltpu.SemaphoreType.DMA
    out = pl.pallas_call(
        functools.partial(dedup_kernel, n, cap),
        out_shape=jax.ShapeDtypeStruct((1, rows), f32),
        in_specs=[pl.BlockSpec(memory_space=pltpu.HBM)] * 2,
        out_specs=pl.BlockSpec(memory_space=pltpu.VMEM),
        scratch_shapes=[
            pltpu.VMEM((rows, width), f32),
            pltpu.VMEM((1, rows), jnp.int32),
            pltpu.VMEM((rows, width), bf16),
            pltpu.VMEM((rows, width), bf16),
            pltpu.VMEM((n, rows), f32),
            pltpu.VMEM((n, cap, width), f32),
            pltpu.VMEM((n, cap, width), f32),
            pltpu.VMEM((planes, LANES, width), bf16),
            pltpu.VMEM((planes, LANES, width), bf16),
            pltpu.VMEM((n, 1, LANES), f32),
            pltpu.VMEM((n, 1, LANES), f32),
            pltpu.VMEM((planes, LANES, LANES), f32),
            pltpu.VMEM((planes, 1, LANES), f32),
            pltpu.VMEM((n, 1, LANES), f32),
            dma((2,)), dma, dma((planes,)), dma, dma, dma, dma,
        ],
        compiler_params=pltpu.CompilerParams(
            collective_id=0, has_side_effects=True, vmem_limit_bytes=54784 * 1024
        ),
    )(embeddings, cluster_ids.reshape(1, rows))
    return out.reshape(rows)


def plain(embeddings, cluster_ids):
    rows, width = embeddings.shape
    owners = lax.axis_size("owners")
    me = lax.axis_index("owners")
    capacity = max(rows * 2 // owners, 2)
    total = owners * capacity
    dest = cluster_ids % owners
    positions = jnp.arange(rows, dtype=jnp.int32)
    same_dest = (dest[:, None] == dest[None, :]) & (positions[None, :] < positions[:, None])
    rank = jnp.sum(same_dest.astype(jnp.int32), axis=1)
    slot_of_row = dest * capacity + rank
    placing = (jnp.arange(total, dtype=jnp.int32)[:, None] == slot_of_row[None, :]).astype(
        jnp.float32
    )
    global_idx = (me * rows + positions).astype(jnp.float32)
    payload = to_unit(embeddings)
    send_rows = jnp.dot(
        placing, payload, precision=lax.Precision.HIGHEST, preferred_element_type=jnp.float32
    ).reshape(owners, capacity, width)
    labels = jnp.stack([global_idx + 1.0, cluster_ids.astype(jnp.float32) + 1.0], axis=1)
    placed_labels = (
        jnp.dot(
            placing, labels, precision=lax.Precision.HIGHEST, preferred_element_type=jnp.float32
        )
        - 1.0
    )
    send_idx = placed_labels[:, 0].reshape(owners, capacity)
    send_clu = placed_labels[:, 1].reshape(owners, capacity)
    got_rows, got_idx, got_clu = (
        lax.all_to_all(send_rows, "owners", split_axis=0, concat_axis=0, tiled=True),
        lax.all_to_all(send_idx, "owners", split_axis=0, concat_axis=0, tiled=True),
        lax.all_to_all(send_clu, "owners", split_axis=0, concat_axis=0, tiled=True),
    )
    flat_rows = got_rows.reshape(total, width)
    flat_idx = got_idx.reshape(total)
    flat_clu = got_clu.reshape(total)
    block = math.gcd(total, 512)

    def one_block(inputs):
        query, query_idx, query_clu = inputs
        scores = jnp.dot(
            query, flat_rows.T, precision=lax.Precision.HIGHEST, preferred_element_type=jnp.float32
        )
        valid = (
            (flat_idx[None, :] >= 0.0)
            & (flat_clu[None, :] == query_clu[:, None])
            & (flat_idx[None, :] < query_idx[:, None])
        )
        return jnp.max(jnp.where(valid, scores, jnp.float32(-1.0)), axis=1)

    best = lax.map(
        one_block,
        (
            flat_rows.reshape(total // block, block, width),
            flat_idx.reshape(total // block, block),
            flat_clu.reshape(total // block, block),
        ),
    )
    back = lax.all_to_all(
        best.reshape(owners, capacity), "owners", split_axis=0, concat_axis=0, tiled=True
    )
    return jnp.dot(
        back.reshape(1, total),
        placing,
        precision=lax.Precision.HIGHEST,
        preferred_element_type=jnp.float32,
    ).reshape(rows)


def shards(embeddings, cluster_ids):
    rows, width = embeddings.shape
    n = lax.axis_size("owners")
    cap = rows * 2 // n
    fits = cap % 8 == 0 and LANES % cap == 0 and n % (LANES // cap) == 0
    if fits and rows % LANES == 0 and width % LANES == 0:
        return fused(embeddings, cluster_ids)
    return plain(embeddings, cluster_ids)


def solution(mesh):
    in_specs = (P(("groups", "owners"), None), P(("groups", "owners")))
    out_specs = P(("groups", "owners"))
    return jax.shard_map(shards, mesh=mesh, in_specs=in_specs, out_specs=out_specs, check_vma=False)
```

```python
import functools
import math

import jax
import jax.numpy as jnp
from jax import lax
from jax.experimental import pallas as pl
from jax.experimental.pallas import tpu as pltpu
from jax.sharding import PartitionSpec as P

LANES = 128
MESH = pl.DeviceIdType.MESH
NT = (((1,), (1,)), ((), ()))
ORDER = (2, 3, 1, 0)


def to_unit(rows):
    return rows / jnp.sqrt(jnp.sum(rows * rows, axis=-1, keepdims=True) + 1e-06)


def split(x):
    high = x.astype(jnp.bfloat16)
    low = (x - high.astype(jnp.float32)).astype(jnp.bfloat16)
    return high, low


def split3(x):
    high, rest = split(x)
    low = x - high.astype(jnp.float32) - rest.astype(jnp.float32)
    return high, rest, low.astype(jnp.bfloat16)


def dedup_kernel(
    n, cap, emb_hbm, clu_hbm, out_ref,
    emb_ref, clu_ref, unit_hi, unit_lo, slot_of, send_rows, got_rows, got_hi, got_lo,
    send_lab, got_lab, lab_col, best, got_best,
    in_sems, row_send, row_recv, lab_send, lab_recv, best_send, best_recv,
):
    rows, width = emb_ref.shape
    per = LANES // cap
    planes = n // per
    me = lax.axis_index("owners")
    my_plane = me // per

    def plane_at(step):
        if planes == 4:
            return lax.bitwise_xor(my_plane, jnp.int32(step))
        return lax.rem(my_plane + step, planes)

    def others(do):
        for step in range(1, n):
            do(lax.rem(me + step, n))

    clu_in = pltpu.make_async_copy(clu_hbm, clu_ref, in_sems.at[0])
    emb_in = pltpu.make_async_copy(emb_hbm, emb_ref, in_sems.at[1])
    barrier = pltpu.get_barrier_semaphore()
    others(
        lambda peer: pl.semaphore_signal(
            barrier, inc=1, device_id={"owners": peer}, device_id_type=MESH
        )
    )

    clu_in.start()
    emb_in.start()

    def remote(src, dst, send, recv, peer):
        return pltpu.make_async_remote_copy(
            src_ref=src, dst_ref=dst, send_sem=send, recv_sem=recv,
            device_id={"owners": peer}, device_id_type=MESH,
        )

    def label_copy(peer):
        return remote(send_lab.at[peer], got_lab.at[me], lab_send, lab_recv, peer)

    def row_copy(peer):
        return remote(
            send_rows.at[peer], got_rows.at[me], row_send, row_recv.at[my_plane], peer
        )

    def best_copy(peer):
        return remote(best.at[peer // per], got_best.at[me], best_send, best_recv, peer)

    def batch(buffer, first, count, send, recv):
        part = buffer.at[pl.ds(first, count)]
        return remote(part, part, send, recv, me)

    clu_in.wait()
    clu = clu_ref[...].astype(jnp.float32)
    label = jnp.floor((clu + 0.5) * (1.0 / n))
    dest = clu - label * n
    label = label + 1.0
    owner = lax.broadcasted_iota(jnp.int32, (n, rows), 0).astype(jnp.float32)
    mine = dest == owner
    member = mine.astype(jnp.bfloat16)
    earlier = (
        lax.broadcasted_iota(jnp.int32, (rows, rows), 0)
        < lax.broadcasted_iota(jnp.int32, (rows, rows), 1)
    ).astype(jnp.bfloat16)
    ranks = jnp.dot(member, earlier, preferred_element_type=jnp.float32)
    slot_of[...] = jnp.where(mine, ranks, -1.0)

    rank = jnp.sum(jnp.where(mine, ranks, 0.0), axis=0, keepdims=True)
    lane_of = lax.broadcasted_iota(jnp.int32, (LANES, rows), 0).astype(jnp.float32)
    placed_labels = lax.dot_general(
        jnp.where(mine, label, 0.0), (lane_of == rank).astype(jnp.float32), NT,
        precision=lax.Precision.HIGHEST, preferred_element_type=jnp.float32,
    )
    for o in range(n):
        send_lab[o] = placed_labels[o : o + 1]

    emb_in.wait()
    unit_hi[...], unit_lo[...] = split(to_unit(emb_ref[...]))

    place = lax.broadcasted_iota(jnp.int32, (cap, rows), 0).astype(jnp.float32)

    def target(step):
        if planes != 4 or step < 2:
            return plane_at(step)
        below = my_plane < 2
        if step == 2:
            return jnp.where(below, 3, 0)
        return jnp.where(below, 2, 1)

    def put(step):
        first = target(step) * per
        placing = jnp.concatenate(
            [(place == slot_of[pl.ds(first + i, 1), :]).astype(jnp.float32) for i in range(per)], axis=0
        ).astype(jnp.bfloat16)
        block = jnp.dot(placing, unit_hi[...], preferred_element_type=jnp.float32) + jnp.dot(
            placing, unit_lo[...], preferred_element_type=jnp.float32
        )
        for i in range(per):
            send_rows[first + i] = block[i * cap : (i + 1) * cap]

    def send(step):
        first = target(step) * per
        if step == 0:
            for i in range(1, per):
                row_copy(first + lax.rem(me - first + i, per)).start()
        else:
            for i in range(per):
                row_copy(first + lax.rem(me + i, per)).start()

    order = ORDER if planes == 4 else tuple(range(planes))[::-1]
    put(order[0])
    pl.semaphore_wait(barrier, n - 1)
    others(lambda peer: label_copy(peer).start())
    got_lab[me] = send_lab[me]
    send(order[0])
    for step in order[1:]:
        put(step)
        send(step)
    got_rows[me] = send_rows[me]

    offset = (lax.rem(me, per) * cap).astype(jnp.float32)
    lookup = (lane_of == rank + offset).astype(jnp.bfloat16)

    batch(got_lab, 0, n - 1, lab_send, lab_recv).wait()
    eye = lax.broadcasted_iota(jnp.int32, (cap, LANES), 0) == lax.broadcasted_iota(
        jnp.int32, (cap, LANES), 1
    )
    for plane in range(planes):
        for i in range(per):
            column = jnp.sum(
                jnp.where(eye, got_lab[plane * per + i], 0.0), axis=1, keepdims=True
            )
            lab_col[plane, pl.ds(i * cap, cap), :] = jnp.broadcast_to(column, (cap, LANES))
        best[plane] = jnp.full((1, LANES), -1.0, jnp.float32)

    def give_back(plane):
        first = plane * per

        @pl.when(plane == my_plane)
        def _():
            for i in range(1, per):
                best_copy(first + lax.rem(me - first + i, per)).start()

        @pl.when(plane != my_plane)
        def _():
            for i in range(per):
                best_copy(first + i).start()

    square = (LANES, LANES)
    row_at = lax.broadcasted_iota(jnp.int32, square, 0)
    lane_at = lax.broadcasted_iota(jnp.int32, square, 1)
    for step in range(planes):
        new = plane_at(step)
        count = per - 1 if step == 0 else per
        batch(got_rows, 0, count, row_send, row_recv.at[new]).wait_recv()
        block = got_rows[pl.ds(new * per, per)].reshape(LANES, width)
        got_hi[new], got_lo[new] = split(block)
        for past in range(step + 1):
            old = plane_at(past)
            low, high = jnp.minimum(old, new), jnp.maximum(old, new)
            scores = (
                lax.dot_general(got_hi[low], got_hi[high], NT, preferred_element_type=jnp.float32)
                + lax.dot_general(got_hi[low], got_lo[high], NT, preferred_element_type=jnp.float32)
                + lax.dot_general(got_lo[low], got_hi[high], NT, preferred_element_type=jnp.float32)
            )
            candidate = lab_col[low]
            query = lab_col[high].T
            valid = (candidate == query) & (candidate > 0.0)
            if past == step:
                valid = valid & (row_at < lane_at)
            top = jnp.max(jnp.where(valid, scores, -1.0), axis=0, keepdims=True)
            best[high] = jnp.maximum(best[high], top)
        if planes == 4 and step == 1:
            @pl.when(my_plane < 2)
            def _():
                give_back(0)
                give_back(1)

    if planes == 4:
        @pl.when(my_plane >= 2)
        def _():
            give_back(0)
            give_back(1)

        give_back(3)
        give_back(2)
    else:
        others(lambda peer: best_copy(peer).start())
    got_best[me] = best[my_plane]
    batch(send_rows, 0, n - 1, row_send, row_recv.at[0]).wait_send()
    batch(got_best, 0, n - 1, best_send, best_recv).wait()

    back = jnp.concatenate([got_best[o] for o in range(n)], axis=0)
    spread = jnp.dot(
        jnp.concatenate(split3(back), axis=0), lookup, preferred_element_type=jnp.float32
    )
    spread = spread[:n] + spread[n : 2 * n] + spread[2 * n :]
    out_ref[...] = jnp.sum(jnp.where(mine, spread, 0.0), axis=0, keepdims=True)


def fused(embeddings, cluster_ids):
    rows, width = embeddings.shape
    n = lax.axis_size("owners")
    cap = rows * 2 // n
    planes = n * cap // LANES
    f32, bf16, dma = jnp.float32, jnp.bfloat16, pltpu.SemaphoreType.DMA
    out = pl.pallas_call(
        functools.partial(dedup_kernel, n, cap),
        out_shape=jax.ShapeDtypeStruct((1, rows), f32),
        in_specs=[pl.BlockSpec(memory_space=pltpu.HBM)] * 2,
        out_specs=pl.BlockSpec(memory_space=pltpu.VMEM),
        scratch_shapes=[
            pltpu.VMEM((rows, width), f32),
            pltpu.VMEM((1, rows), jnp.int32),
            pltpu.VMEM((rows, width), bf16),
            pltpu.VMEM((rows, width), bf16),
            pltpu.VMEM((n, rows), f32),
            pltpu.VMEM((n, cap, width), f32),
            pltpu.VMEM((n, cap, width), f32),
            pltpu.VMEM((planes, LANES, width), bf16),
            pltpu.VMEM((planes, LANES, width), bf16),
            pltpu.VMEM((n, 1, LANES), f32),
            pltpu.VMEM((n, 1, LANES), f32),
            pltpu.VMEM((planes, LANES, LANES), f32),
            pltpu.VMEM((planes, 1, LANES), f32),
            pltpu.VMEM((n, 1, LANES), f32),
            dma((2,)), dma, dma((planes,)), dma, dma, dma, dma,
        ],
        compiler_params=pltpu.CompilerParams(
            collective_id=0, has_side_effects=True, vmem_limit_bytes=54784 * 1024
        ),
    )(embeddings, cluster_ids.reshape(1, rows))
    return out.reshape(rows)


def plain(embeddings, cluster_ids):
    rows, width = embeddings.shape
    owners = lax.axis_size("owners")
    me = lax.axis_index("owners")
    capacity = max(rows * 2 // owners, 2)
    total = owners * capacity
    dest = cluster_ids % owners
    positions = jnp.arange(rows, dtype=jnp.int32)
    same_dest = (dest[:, None] == dest[None, :]) & (positions[None, :] < positions[:, None])
    rank = jnp.sum(same_dest.astype(jnp.int32), axis=1)
    slot_of_row = dest * capacity + rank
    placing = (jnp.arange(total, dtype=jnp.int32)[:, None] == slot_of_row[None, :]).astype(
        jnp.float32
    )
    global_idx = (me * rows + positions).astype(jnp.float32)
    payload = to_unit(embeddings)
    send_rows = jnp.dot(
        placing, payload, precision=lax.Precision.HIGHEST, preferred_element_type=jnp.float32
    ).reshape(owners, capacity, width)
    labels = jnp.stack([global_idx + 1.0, cluster_ids.astype(jnp.float32) + 1.0], axis=1)
    placed_labels = (
        jnp.dot(
            placing, labels, precision=lax.Precision.HIGHEST, preferred_element_type=jnp.float32
        )
        - 1.0
    )
    send_idx = placed_labels[:, 0].reshape(owners, capacity)
    send_clu = placed_labels[:, 1].reshape(owners, capacity)
    got_rows, got_idx, got_clu = (
        lax.all_to_all(send_rows, "owners", split_axis=0, concat_axis=0, tiled=True),
        lax.all_to_all(send_idx, "owners", split_axis=0, concat_axis=0, tiled=True),
        lax.all_to_all(send_clu, "owners", split_axis=0, concat_axis=0, tiled=True),
    )
    flat_rows = got_rows.reshape(total, width)
    flat_idx = got_idx.reshape(total)
    flat_clu = got_clu.reshape(total)
    block = math.gcd(total, 512)

    def one_block(inputs):
        query, query_idx, query_clu = inputs
        scores = jnp.dot(
            query, flat_rows.T, precision=lax.Precision.HIGHEST, preferred_element_type=jnp.float32
        )
        valid = (
            (flat_idx[None, :] >= 0.0)
            & (flat_clu[None, :] == query_clu[:, None])
            & (flat_idx[None, :] < query_idx[:, None])
        )
        return jnp.max(jnp.where(valid, scores, jnp.float32(-1.0)), axis=1)

    best = lax.map(
        one_block,
        (
            flat_rows.reshape(total // block, block, width),
            flat_idx.reshape(total // block, block),
            flat_clu.reshape(total // block, block),
        ),
    )
    back = lax.all_to_all(
        best.reshape(owners, capacity), "owners", split_axis=0, concat_axis=0, tiled=True
    )
    return jnp.dot(
        back.reshape(1, total),
        placing,
        precision=lax.Precision.HIGHEST,
        preferred_element_type=jnp.float32,
    ).reshape(rows)


def shards(embeddings, cluster_ids):
    rows, width = embeddings.shape
    n = lax.axis_size("owners")
    cap = rows * 2 // n
    fits = cap % 8 == 0 and LANES % cap == 0 and n % (LANES // cap) == 0
    if fits and rows % LANES == 0 and width % LANES == 0:
        return fused(embeddings, cluster_ids)
    return plain(embeddings, cluster_ids)


def solution(mesh):
    in_specs = (P(("groups", "owners"), None), P(("groups", "owners")))
    out_specs = P(("groups", "owners"))
    return jax.shard_map(shards, mesh=mesh, in_specs=in_specs, out_specs=out_specs, check_vma=False)
```
